512 devices in a mesh: seq: 64 (over x, z_lo, core), kvh: 8 (over z_hi, y).
Axes of the slice: x: 4, y: 4, z: 16 (z_hi: 2, z_lo: 8; z = z_hi * 8 + z_lo), core: 2. Of those that a mesh axis runs over, the one named last changes fastest.
Arguments:
- queries: bfloat16 [16384, 12288], P('seq', 'kvh'), may hold values from -4 to 4
- keys: bfloat16 [16384, 1024], P('seq', 'kvh'), may hold values from -10 to 10
- values: bfloat16 [16384, 1024], P('seq', 'kvh'), may hold values from -6 to 6
- answer_lengths: int32 [16], replicated, may hold values from 512 to 3072, as said below
Outputs:
- attended: bfloat16 [16384, 12288], P(('seq', 'kvh'))
The draws below stay inside these ranges and needn't reach their ends.
Inputs may be any that keep to these rules, and one draw needn't show every extreme that they name: `answer_lengths`: every length is a multiple of 256; the lengths sum to 16384; exactly one answer has the largest length 3072, every other one at most (11) * 256.
All inputs are finite; a program needn't handle non-finite values.
Results may differ from the reference program's by a relative error of at most 0.0035.
Values may be sent and summed in bfloat16 or wider, within the bound.
A program may use at most 64 MiB of HBM per device.

```python
import math
import jax
import jax.numpy as jnp
from jax import lax

KEY_VALUE_HEADS = 8
QUERY_PER_KEY = 12
HEAD_WIDTH = 128
TOKENS_PER_SHARD = 256
PACKED_TOKENS = 16384
SPAN_MOST = 12
ANSWERS = 16
N_SEQ = 64


def draw_queries(key, part):
    key = jax.random.fold_in(key, 11)
    table_items = jax.random.truncated_normal(key, -4.0, 4.0, (PACKED_TOKENS, KEY_VALUE_HEADS * QUERY_PER_KEY * HEAD_WIDTH), jnp.float32)
    return table_items.astype(jnp.bfloat16)


def draw_keys(key, part):
    key = jax.random.fold_in(key, 23)
    table_items = 2.5 * jax.random.truncated_normal(key, -4.0, 4.0, (PACKED_TOKENS, KEY_VALUE_HEADS * HEAD_WIDTH), jnp.float32)
    return table_items.astype(jnp.bfloat16)


def draw_answer_lengths(key, part):
    key = jax.random.fold_in(key, 5)
    pick_key, order_key = jax.random.split(key)
    others = ANSWERS - 1
    extra_units = N_SEQ - SPAN_MOST - 2 * others
    room = SPAN_MOST - 3
    picks = jax.random.randint(pick_key, (max(extra_units, 1),), 0, others)

    def place_unit(unit_index, counts):
        wanted = picks[unit_index]
        crowded = counts[wanted] >= room
        emptiest = jnp.argmin(counts).astype(jnp.int32)
        target = jnp.where(crowded, emptiest, wanted)
        return counts.at[target].add(1)
    counts = lax.fori_loop(0, extra_units, place_unit, jnp.zeros((others,), jnp.int32))
    spans = jnp.concatenate([counts + 2, jnp.full((1,), SPAN_MOST, jnp.int32)])
    order = jax.random.permutation(order_key, ANSWERS)
    spans = spans[order]
    return (spans * TOKENS_PER_SHARD).astype(jnp.int32)


def shard_levels(stream_key, dims, cuts, least, largest):
    factor_of = 1.0
    for position, shards_of in cuts:
        steps = jax.random.uniform(jax.random.fold_in(jax.random.fold_in(stream_key, 6), position), (shards_of,), jnp.float32, least / len(cuts), largest / len(cuts))
        factor_of = factor_of * jnp.repeat(jnp.exp(steps), dims[position] // shards_of).reshape((-1,) + (1,) * (len(dims) - 1 - position))
    return factor_of


def bell_draw(own_key, dims, deviation, reach, shards=(), kind=jnp.bfloat16):
    entries = jax.random.normal(own_key, dims, jnp.float32) * deviation
    if len(shards) > 0:
        entries = shard_levels(own_key, dims, shards, -0.22, 0.18) * entries
    return jnp.clip(entries, min=-reach, max=reach).astype(kind)


def setup_inputs(seed: int = 0) -> dict:
    splits = jax.random.split(jax.random.key(seed), 5)
    return {
        "queries": draw_queries(jax.random.fold_in(splits[4], 71), 0),
        "keys": draw_keys(jax.random.fold_in(splits[4], 71), 0),
        "values": bell_draw(splits[2], (PACKED_TOKENS, KEY_VALUE_HEADS * HEAD_WIDTH), 1.0, 6.0, ((0, 64), (1, 8))),
        "answer_lengths": draw_answer_lengths(jax.random.fold_in(splits[4], 71), 0),
    }


def reference(queries, keys, values, answer_lengths):
    every_token = queries.shape[0]
    token_count = every_token // N_SEQ
    visible_span = SPAN_MOST * token_count
    answer_starts = jnp.cumsum(answer_lengths, dtype=jnp.int32) - answer_lengths
    answer_ends = answer_starts + answer_lengths
    positions = jnp.arange(every_token, dtype=jnp.int32)
    holding = (answer_starts[None, :] <= positions[:, None]) & (positions[:, None] < answer_ends[None, :])
    first_tokens = lax.optimization_barrier(jnp.sum(jnp.where(holding, answer_starts[None, :], 0), axis=1)).astype(jnp.int32)
    score_scale = 1.0 / math.sqrt(HEAD_WIDTH)

    def one_block(block_index):
        query_start = (block_index * token_count).astype(jnp.int32)
        key_begin = jnp.clip(query_start - (SPAN_MOST - 1) * token_count, 0, every_token - visible_span).astype(jnp.int32)
        query_matrix = lax.dynamic_slice_in_dim(queries, query_start, token_count, 0).astype(jnp.float32)
        query_matrix = query_matrix.reshape(token_count, KEY_VALUE_HEADS, QUERY_PER_KEY, HEAD_WIDTH)
        key_matrix = lax.dynamic_slice_in_dim(keys, key_begin, visible_span, 0).astype(jnp.float32).reshape(visible_span, KEY_VALUE_HEADS, HEAD_WIDTH)
        value_matrix = lax.dynamic_slice_in_dim(values, key_begin, visible_span, 0).astype(jnp.float32).reshape(visible_span, KEY_VALUE_HEADS, HEAD_WIDTH)
        query_pos = query_start + jnp.arange(token_count, dtype=jnp.int32)
        key_pos = key_begin + jnp.arange(visible_span, dtype=jnp.int32)
        query_first = lax.dynamic_slice_in_dim(first_tokens, query_start, token_count, 0)
        visible = (key_pos[None, :] <= query_pos[:, None]) & (key_pos[None, :] >= query_first[:, None])
        visible_grid = visible[None, :, None, :]
        scores = jnp.einsum('tkgd,wkd->ktgw', query_matrix, key_matrix) * score_scale
        row_max = lax.optimization_barrier(jnp.max(jnp.where(visible_grid, scores, -jnp.inf), axis=-1))
        probs = jnp.exp(jnp.where(visible_grid, scores - row_max[..., None], -jnp.inf))
        row_total = lax.optimization_barrier(jnp.sum(probs, axis=-1))
        weights = lax.optimization_barrier(probs.astype(jnp.bfloat16)).astype(jnp.float32)
        blended = jnp.einsum('ktgw,wkd->tkgd', weights, value_matrix)
        blended = blended / jnp.transpose(row_total, (1, 0, 2))[..., None]
        return blended.astype(jnp.bfloat16).reshape(token_count, KEY_VALUE_HEADS * QUERY_PER_KEY * HEAD_WIDTH)
    block_list = lax.map(one_block, jnp.arange(N_SEQ, dtype=jnp.int32))
    return block_list.reshape(every_token, KEY_VALUE_HEADS * QUERY_PER_KEY * HEAD_WIDTH)
```

```python
import functools
import math

import jax
import jax.numpy as jnp
from jax import lax
from jax.experimental import pallas as pl
from jax.experimental.pallas import tpu as pltpu
from jax.sharding import PartitionSpec as P

HEAD = 128
SPAN = 12
MESH = pl.DeviceIdType.MESH
LOW = -1e30
EXP2_SCALE = math.log2(math.e) / math.sqrt(HEAD)


def kernel(n_seq, n_kvh, len_ref, q_hbm, k_hbm, v_hbm, out_hbm, qv, kv, s_scr, stage,
           local_sem, main_send, main_recv, aux_send, aux_recv, out_send, out_recv):
    tokens, width = qv.shape
    heads = width // HEAD
    rows = tokens // n_kvh
    half = n_kvh // 2
    me = lax.axis_index("seq")
    mine = lax.axis_index("kvh")
    core = lax.rem(me, 2)
    my_hi = mine // half
    my_lo = lax.rem(mine, half)

    def seq_at(step):
        return lax.rem(me + (step + n_seq), n_seq)

    def peer(i):
        cross = i < half
        hi = jnp.where(cross, 1 - my_hi, my_hi)
        lo = lax.rem(my_lo + jnp.where(cross, i, i - half + 1), half)
        return hi * half + lo

    local = [
        pltpu.make_async_copy(k_hbm, kv.at[0, 0], local_sem.at[0]),
        pltpu.make_async_copy(v_hbm, kv.at[0, 1], local_sem.at[1]),
        pltpu.make_async_copy(q_hbm, qv, local_sem.at[2]),
    ]
    for copy in local:
        copy.start()

    barrier = pltpu.get_barrier_semaphore()
    for step in (-2, -1, 1, 2):
        pl.semaphore_signal(barrier, inc=1, device_id={"seq": seq_at(step)}, device_id_type=MESH)
    for i in range(n_kvh - 1):
        pl.semaphore_signal(barrier, inc=1, device_id={"kvh": peer(i)}, device_id_type=MESH)

    base = me * tokens
    first = jnp.int32(0)
    start = jnp.int32(0)
    for a in range(len_ref.shape[0]):
        first = jnp.where(start <= base, start, first)
        start = start + len_ref[a]

    local[0].wait()
    local[1].wait()
    pl.semaphore_wait(barrier, 4 + n_kvh - 1)

    def main_copy(t, part):
        return pltpu.make_async_remote_copy(
            src_ref=kv.at[2 * t, part], dst_ref=kv.at[2 * t + 2, part],
            send_sem=main_send.at[t, part], recv_sem=main_recv.at[t, part],
            device_id={"seq": seq_at(2)}, device_id_type=MESH)

    def aux_copy(u, part, src, step):
        return pltpu.make_async_remote_copy(
            src_ref=kv.at[src, part], dst_ref=kv.at[2 * u + 1, part],
            send_sem=aux_send.at[u, part], recv_sem=aux_recv.at[u, part],
            device_id={"seq": seq_at(step)}, device_id_type=MESH)

    for t in range(SPAN // 2):
        for part in range(2):
            if t > 0:
                main_copy(t - 1, part).wait_recv()
            if t < SPAN // 2 - 1:
                main_copy(t, part).start()

            @pl.when(core == 0)
            def _():
                aux_copy(t, part, 2 * t, 1).start()

            if t > 0:
                @pl.when(core == 1)
                def _():
                    aux_copy(t - 1, part, 2 * t, -1).start()
            if t == SPAN // 2 - 1:
                @pl.when(core == 1)
                def _():
                    aux_copy(t, part, 2 * t, 1).start()

    for u in range(SPAN // 2):
        for part in range(2):
            aux_copy(u, part, 0, 1).wait_recv()
    local[2].wait()

    def attend(row0):
        q = jnp.concatenate(
            [qv[pl.ds(row0, rows), h * HEAD:(h + 1) * HEAD] for h in range(heads)], axis=0)
        peak = jnp.full((heads * rows, HEAD), LOW, jnp.float32)
        for b in range(SPAN):
            s = lax.dot_general(q, kv[b, 0], (((1,), (1,)), ((), ())),
                                preferred_element_type=jnp.float32)
            if b == 0:
                token = row0 + lax.rem(lax.broadcasted_iota(jnp.int32, s.shape, 0), rows)
                s = jnp.where(lax.broadcasted_iota(jnp.int32, s.shape, 1) <= token, s, LOW)
            s_scr[:, b * tokens:(b + 1) * tokens] = s
            best = s[:, :HEAD]
            for j in range(1, tokens // HEAD):
                best = jnp.maximum(best, s[:, j * HEAD:(j + 1) * HEAD])
            if b > 0:
                best = jnp.where(b * tokens <= base - first, best, LOW)
            peak = jnp.maximum(peak, best)
        peak = jnp.max(peak, axis=1, keepdims=True)
        total = jnp.zeros((heads * rows, HEAD), jnp.float32)
        acc = jnp.zeros((heads * rows, HEAD), jnp.float32)
        for b in range(SPAN):
            shift = peak if b == 0 else jnp.where(b * tokens <= base - first, peak, -LOW)
            p = jnp.exp2((s_scr[:, b * tokens:(b + 1) * tokens] - shift) * EXP2_SCALE)
            for j in range(tokens // HEAD):
                total = total + p[:, j * HEAD:(j + 1) * HEAD]
            acc = acc + jnp.dot(p.astype(jnp.bfloat16), kv[b, 1], preferred_element_type=jnp.float32)
        return (acc / jnp.sum(total, axis=1, keepdims=True)).astype(jnp.bfloat16)

    def out_copy(i):
        columns = pl.ds(pl.multiple_of(mine * width, width), width)
        return pltpu.make_async_remote_copy(
            src_ref=stage.at[i], dst_ref=out_hbm.at[:, columns],
            send_sem=out_send.at[i], recv_sem=out_recv.at[i],
            device_id={"kvh": peer(i)}, device_id_type=MESH)

    def self_copy():
        columns = pl.ds(pl.multiple_of(mine * width, width), width)
        return pltpu.make_async_copy(stage.at[n_kvh - 1], out_hbm.at[:, columns], local_sem.at[3])

    def one_chunk(i, carry):
        target = jnp.where(i == n_kvh - 1, mine, peer(i))
        done = attend(pl.multiple_of(target * rows, rows))
        for h in range(heads):
            stage[i, :, h * HEAD:(h + 1) * HEAD] = done[h * rows:(h + 1) * rows, :]

        @pl.when(i < n_kvh - 1)
        def _():
            out_copy(i).start()

        return carry

    lax.fori_loop(0, n_kvh, one_chunk, 0)
    self_copy().start()
    self_copy().wait()
    for i in range(n_kvh - 1):
        out_copy(i).wait()
    for t in range(SPAN // 2):
        for part in range(2):
            if t < SPAN // 2 - 1:
                main_copy(t, part).wait_send()
            aux_copy(t, part, 0, 1).wait_send()


def shards(queries, keys, values, answer_lengths):
    tokens, width = queries.shape
    n_seq, n_kvh = lax.axis_size("seq"), lax.axis_size("kvh")
    rows = tokens // n_kvh
    heads = width // HEAD
    dma = pltpu.SemaphoreType.DMA
    any_spec = pl.BlockSpec(memory_space=pl.ANY)
    return pl.pallas_call(
        functools.partial(kernel, n_seq, n_kvh),
        out_shape=jax.ShapeDtypeStruct((rows, n_kvh * width), jnp.bfloat16),
        in_specs=[pl.BlockSpec(memory_space=pltpu.SMEM), any_spec, any_spec, any_spec],
        out_specs=any_spec,
        scratch_shapes=[
            pltpu.VMEM((tokens, width), jnp.bfloat16),
            pltpu.VMEM((SPAN, 2, tokens, HEAD), jnp.bfloat16),
            pltpu.VMEM((heads * rows, SPAN * tokens), jnp.float32),
            pltpu.VMEM((n_kvh, rows, width), jnp.bfloat16),
            dma((4,)),
            dma((SPAN // 2, 2)),
            dma((SPAN // 2, 2)),
            dma((SPAN // 2, 2)),
            dma((SPAN // 2, 2)),
            dma((n_kvh,)),
            dma((n_kvh,)),
        ],
        compiler_params=pltpu.CompilerParams(
            collective_id=0, has_side_effects=True, vmem_limit_bytes=48 * 1024 * 1024),
        cost_estimate=pl.CostEstimate(
            flops=4 * tokens * width * SPAN * tokens,
            bytes_accessed=4 * tokens * width,
            transcendentals=tokens * heads * SPAN * tokens),
    )(answer_lengths, queries, keys, values)


def solution(mesh):
    in_specs = (P("seq", "kvh"), P("seq", "kvh"), P("seq", "kvh"), P())
    out_specs = P(("seq", "kvh"), None)
    return jax.shard_map(shards, mesh=mesh, in_specs=in_specs, out_specs=out_specs, check_vma=False)
```

```python
import functools
import math

import jax
import jax.numpy as jnp
from jax import lax
from jax.experimental import pallas as pl
from jax.experimental.pallas import tpu as pltpu
from jax.sharding import PartitionSpec as P

HEAD = 128
SPAN = 12
PARTS = 4
RUN = 8
MESH = pl.DeviceIdType.MESH
LOW = -1e30
EXP2_SCALE = math.log2(math.e) / math.sqrt(HEAD)


def kernel(n_seq, n_kvh, len_hbm, q_hbm, k_hbm, v_hbm, out_hbm, lens, qv, kv, s_scr, stage, peak_scr, total_scr, acc_scr,
           local_sem, main_send, main_recv, aux_send, aux_recv, out_send, out_recv, ready):
    tokens, width = qv.shape
    heads = width // HEAD
    rows = tokens // n_kvh
    half = n_kvh // 2
    me = lax.axis_index("seq")
    mine = lax.axis_index("kvh")
    core = lax.rem(me, 2)
    my_hi = mine // half
    my_lo = lax.rem(mine, half)

    def seq_at(step):
        return lax.rem(me + (step + n_seq), n_seq)

    def peer(r):
        cross = r < half
        hi = jnp.where(cross, 1 - my_hi, my_hi)
        lo = lax.rem(my_lo + jnp.where(cross, r, r - half + 1), half)
        return hi * half + lo

    local = [
        pltpu.make_async_copy(k_hbm, kv.at[0, :tokens], local_sem.at[0]),
        pltpu.make_async_copy(v_hbm, kv.at[0, tokens:], local_sem.at[1]),
        pltpu.make_async_copy(q_hbm, qv, local_sem.at[2]),
        pltpu.make_async_copy(len_hbm, lens, local_sem.at[3]),
    ]
    for copy in local:
        copy.start()

    barrier = pltpu.get_barrier_semaphore()
    for step in (-2, -1, 1, 2):
        pl.semaphore_signal(barrier, inc=1, device_id={"seq": seq_at(step)}, device_id_type=MESH)
    for r in range(half, n_kvh - 1):
        pl.semaphore_signal(barrier, inc=1, device_id={"kvh": peer(r)}, device_id_type=MESH)

    @pl.when(my_hi == 0)
    def _():
        for r in range(half):
            pl.semaphore_signal(barrier, inc=1, device_id={"kvh": peer(r)}, device_id_type=MESH)

    local[0].wait()
    local[1].wait()
    pl.semaphore_wait(barrier, 4 + (half - 1) + my_hi * half)

    @pl.when(my_hi == 1)
    def _():
        for r in range(half):
            pl.semaphore_signal(ready, inc=1, device_id={"kvh": peer(r)}, device_id_type=MESH)


    piece = 2 * tokens // PARTS

    def main_copy(t, part):
        span = pl.ds(part * piece, piece)
        return pltpu.make_async_remote_copy(
            src_ref=kv.at[2 * t, span], dst_ref=kv.at[2 * t + 2, span],
            send_sem=main_send.at[t, part], recv_sem=main_recv.at[t, part],
            device_id={"seq": seq_at(2)}, device_id_type=MESH)

    def aux_copy(u, part, src, step):
        span = pl.ds(part * piece, piece)
        return pltpu.make_async_remote_copy(
            src_ref=kv.at[src, span], dst_ref=kv.at[2 * u + 1, span],
            send_sem=aux_send.at[u, part], recv_sem=aux_recv.at[u, part],
            device_id={"seq": seq_at(step)}, device_id_type=MESH)

    far = lax.rem(me // 2, RUN) >= RUN // 2
    first_r = jnp.where(far, half, 0)
    lead_row = pl.multiple_of(peer(first_r) * rows, rows)
    group = heads // PARTS

    def seen(b):
        return b * tokens <= base - first

    def lead(blocks, part):
        fresh = blocks[0] == 0
        where = pl.ds(part * group * rows, group * rows)
        q = jnp.concatenate(
            [qv[pl.ds(lead_row, rows), h * HEAD:(h + 1) * HEAD]
             for h in range(part * group, (part + 1) * group)], axis=0)
        scores = []
        for b in blocks:
            s = lax.dot_general(q, kv[b, :tokens], (((1,), (1,)), ((), ())),
                                preferred_element_type=jnp.float32)
            if b == 0:
                token = lead_row + lax.rem(lax.broadcasted_iota(jnp.int32, s.shape, 0), rows)
                s = jnp.where(lax.broadcasted_iota(jnp.int32, s.shape, 1) <= token, s, LOW)
            scores.append(s)
        old = jnp.full((group * rows, HEAD), LOW, jnp.float32) if fresh else peak_scr[where, :]
        best = old[:, :1]
        for b, s in zip(blocks, scores):
            top = jnp.max(s, axis=1, keepdims=True)
            best = jnp.maximum(best, top if b == 0 else jnp.where(seen(b), top, LOW))
        total = jnp.zeros((group * rows, HEAD), jnp.float32)
        acc = jnp.zeros((group * rows, HEAD), jnp.float32)
        for b, s in zip(blocks, scores):
            shift = best if b == 0 else jnp.where(seen(b), best, -LOW)
            p = jnp.exp2((s - shift) * EXP2_SCALE)
            for j in range(tokens // HEAD):
                total = total + p[:, j * HEAD:(j + 1) * HEAD]
            acc = acc + jnp.dot(p.astype(jnp.bfloat16), kv[b, tokens:], preferred_element_type=jnp.float32)
        if not fresh:
            shrink = jnp.exp2((old - best) * EXP2_SCALE)
            total = total + total_scr[where, :] * shrink
            acc = acc + acc_scr[where, :] * shrink
        peak_scr[where, :] = jnp.broadcast_to(best, (group * rows, HEAD))
        total_scr[where, :] = total
        acc_scr[where, :] = acc

    def aux_wait(u):
        for part in range(PARTS):
            aux_copy(u, part, 0, 1).wait_recv()

    for t in range(SPAN // 2):
        for part in range(PARTS):
            if t > 0:
                main_copy(t - 1, part).wait_recv()
            if t < SPAN // 2 - 1:
                main_copy(t, part).start()

            @pl.when(core == 0)
            def _():
                aux_copy(t, part, 2 * t, 1).start()

            if t > 0:
                @pl.when(core == 1)
                def _():
                    aux_copy(t - 1, part, 2 * t, -1).start()
            if t == SPAN // 2 - 1:
                @pl.when(core == 1)
                def _():
                    aux_copy(t, part, 2 * t, 1).start()
            if t > 0:
                if t > 1 and part == 0:
                    aux_wait(t - 2)
                lead((0,) if t == 1 else (2 * t - 2, 2 * t - 3), part)
        if t == 0:
            local[2].wait()
            local[3].wait()
            base = me * tokens
            first = jnp.int32(0)
            start = jnp.int32(0)
            for a in range(lens.shape[0]):
                first = jnp.where(start <= base, start, first)
                start = start + lens[a]

    for blocks in ((SPAN - 2, SPAN - 3), (SPAN - 1,)):
        aux_wait((blocks[-1] - 1) // 2)
        for part in range(PARTS):
            lead(blocks, part)

    def attend(row0):
        q = jnp.concatenate(
            [qv[pl.ds(row0, rows), h * HEAD:(h + 1) * HEAD] for h in range(heads)], axis=0)
        peak = jnp.full((heads * rows, HEAD), LOW, jnp.float32)
        for b in range(SPAN):
            s = lax.dot_general(q, kv[b, :tokens], (((1,), (1,)), ((), ())),
                                preferred_element_type=jnp.float32)
            if b == 0:
                token = row0 + lax.rem(lax.broadcasted_iota(jnp.int32, s.shape, 0), rows)
                s = jnp.where(lax.broadcasted_iota(jnp.int32, s.shape, 1) <= token, s, LOW)
            s_scr[:, b * tokens:(b + 1) * tokens] = s
            best = s[:, :HEAD]
            for j in range(1, tokens // HEAD):
                best = jnp.maximum(best, s[:, j * HEAD:(j + 1) * HEAD])
            if b > 0:
                best = jnp.where(seen(b), best, LOW)
            peak = jnp.maximum(peak, best)
        peak = jnp.max(peak, axis=1, keepdims=True)
        total = jnp.zeros((heads * rows, HEAD), jnp.float32)
        acc = jnp.zeros((heads * rows, HEAD), jnp.float32)
        for b in range(SPAN):
            shift = peak if b == 0 else jnp.where(seen(b), peak, -LOW)
            p = jnp.exp2((s_scr[:, b * tokens:(b + 1) * tokens] - shift) * EXP2_SCALE)
            for j in range(tokens // HEAD):
                total = total + p[:, j * HEAD:(j + 1) * HEAD]
            acc = acc + jnp.dot(p.astype(jnp.bfloat16), kv[b, tokens:], preferred_element_type=jnp.float32)
        return (acc / jnp.sum(total, axis=1, keepdims=True)).astype(jnp.bfloat16)

    columns = pl.ds(pl.multiple_of(mine * width, width), width)

    def out_copy(r):
        return pltpu.make_async_remote_copy(
            src_ref=stage.at[r], dst_ref=out_hbm.at[:, columns],
            send_sem=out_send.at[r], recv_sem=out_recv.at[r],
            device_id={"kvh": peer(r)}, device_id_type=MESH)

    def finish(r, done):
        for h in range(heads):
            stage[r, :, h * HEAD:(h + 1) * HEAD] = done[h * rows:(h + 1) * rows, :]

        @pl.when(r < n_kvh - 1)
        def _():
            out_copy(r).start()

    @pl.when(my_hi == 0)
    def _():
        pl.semaphore_wait(ready, half)

    finish(first_r, (acc_scr[...] / jnp.sum(total_scr[...], axis=1, keepdims=True)).astype(jnp.bfloat16))

    def one_chunk(i, carry):
        r = lax.rem(i + first_r, n_kvh)
        target = jnp.where(r == n_kvh - 1, mine, peer(r))
        finish(r, attend(pl.multiple_of(target * rows, rows)))
        return carry

    lax.fori_loop(1, n_kvh, one_chunk, 0)
    self_copy = pltpu.make_async_copy(stage.at[n_kvh - 1], out_hbm.at[:, columns], local_sem.at[0])
    self_copy.start()
    self_copy.wait()
    for r in range(n_kvh - 1):
        out_copy(r).wait()
    for t in range(SPAN // 2):
        for part in range(PARTS):
            if t < SPAN // 2 - 1:
                main_copy(t, part).wait_send()
            aux_copy(t, part, 0, 1).wait_send()


def shards(queries, keys, values, answer_lengths):
    tokens, width = queries.shape
    n_seq, n_kvh = lax.axis_size("seq"), lax.axis_size("kvh")
    rows = tokens // n_kvh
    heads = width // HEAD
    dma = pltpu.SemaphoreType.DMA
    hbm_spec = pl.BlockSpec(memory_space=pltpu.HBM)
    return pl.pallas_call(
        functools.partial(kernel, n_seq, n_kvh),
        out_shape=jax.ShapeDtypeStruct((rows, n_kvh * width), jnp.bfloat16),
        in_specs=[hbm_spec] * 4,
        out_specs=pl.BlockSpec(memory_space=pl.ANY),
        scratch_shapes=[
            pltpu.SMEM(answer_lengths.shape, jnp.int32),
            pltpu.VMEM((tokens, width), jnp.bfloat16),
            pltpu.VMEM((SPAN, 2 * tokens, HEAD), jnp.bfloat16),
            pltpu.VMEM((heads * rows, SPAN * tokens), jnp.float32),
            pltpu.VMEM((n_kvh, rows, width), jnp.bfloat16),
            pltpu.VMEM((heads * rows, HEAD), jnp.float32),
            pltpu.VMEM((heads * rows, HEAD), jnp.float32),
            pltpu.VMEM((heads * rows, HEAD), jnp.float32),
            dma((4,)),
            dma((SPAN // 2, PARTS)),
            dma((SPAN // 2, PARTS)),
            dma((SPAN // 2, PARTS)),
            dma((SPAN // 2, PARTS)),
            dma((n_kvh,)),
            dma((n_kvh,)),
            pltpu.SemaphoreType.REGULAR,
        ],
        compiler_params=pltpu.CompilerParams(
            collective_id=0, has_side_effects=True, vmem_limit_bytes=63 * 1024 * 1024),
        cost_estimate=pl.CostEstimate(
            flops=4 * tokens * width * SPAN * tokens,
            bytes_accessed=4 * tokens * width,
            transcendentals=tokens * heads * SPAN * tokens),
    )(answer_lengths, queries, keys, values)


def solution(mesh):
    in_specs = (P("seq", "kvh"), P("seq", "kvh"), P("seq", "kvh"), P())
    out_specs = P(("seq", "kvh"), None)
    return jax.shard_map(shards, mesh=mesh, in_specs=in_specs, out_specs=out_specs, check_vma=False)
```

```python
import functools
import math

import jax
import jax.numpy as jnp
from jax import lax
from jax.experimental import pallas as pl
from jax.experimental.pallas import tpu as pltpu
from jax.sharding import PartitionSpec as P

HEAD = 128
SPAN = 12
PARTS = 4
RUN = 8
FAR_STEP = (0, 1, 1, 2, 2)
MESH = pl.DeviceIdType.MESH
LOW = -1e30
EXP2_SCALE = math.log2(math.e) / math.sqrt(HEAD)


def kernel(n_seq, n_kvh, len_hbm, q_hbm, k_hbm, v_hbm, out_hbm, lens, qv, kv, s_scr, stage, peak_scr, total_scr, acc_scr,
           local_sem, main_send, main_recv, aux_send, aux_recv, far_send, out_send, out_recv, ready):
    tokens, width = qv.shape
    heads = width // HEAD
    rows = tokens // n_kvh
    half = n_kvh // 2
    me = lax.axis_index("seq")
    mine = lax.axis_index("kvh")
    core = lax.rem(me, 2)
    chip = lax.rem(me // 2, RUN)
    last = SPAN // 2 - 1
    my_hi = mine // half
    my_lo = lax.rem(mine, half)

    def seq_at(step):
        return lax.rem(me + (step + n_seq), n_seq)

    def peer(r):
        cross = r < half
        hi = jnp.where(cross, 1 - my_hi, my_hi)
        lo = lax.rem(my_lo + jnp.where(cross, r, r - half + 1), half)
        return hi * half + lo

    local = [
        pltpu.make_async_copy(k_hbm, kv.at[0, :tokens], local_sem.at[0]),
        pltpu.make_async_copy(v_hbm, kv.at[0, tokens:], local_sem.at[1]),
        pltpu.make_async_copy(q_hbm, qv, local_sem.at[2]),
        pltpu.make_async_copy(len_hbm, lens, local_sem.at[3]),
    ]
    for copy in local:
        copy.start()

    barrier = pltpu.get_barrier_semaphore()
    greets = [(-2, core >= 0), (1 - 2 * core, core >= 0), (-1, (core == 0) & (chip > 0))]
    greets += [(-2 * m, chip == 0) for m in range(2, last + 1)]
    greets += [(-2 * last - 1, (core == 0) & (chip == 0))]
    for step, known in greets:
        @pl.when(known)
        def _():
            pl.semaphore_signal(barrier, inc=1, device_id={"seq": seq_at(step)}, device_id_type=MESH)
    tail = (core == 1) & (chip < RUN - 1)
    far_even = (chip >= RUN - last) & (chip < RUN - 1)
    far_odd = (core == 1) & (chip == RUN - last - 1)
    greeted = half - 1 + my_hi * half + 2
    for known in (tail, far_even, far_odd):
        greeted = greeted + known.astype(jnp.int32)

    for r in range(half, n_kvh - 1):
        pl.semaphore_signal(barrier, inc=1, device_id={"kvh": peer(r)}, device_id_type=MESH)

    @pl.when(my_hi == 0)
    def _():
        for r in range(half):
            pl.semaphore_signal(barrier, inc=1, device_id={"kvh": peer(r)}, device_id_type=MESH)

    local[0].wait()
    local[1].wait()
    pl.semaphore_wait(barrier, greeted)

    @pl.when(my_hi == 1)
    def _():
        for r in range(half):
            pl.semaphore_signal(ready, inc=1, device_id={"kvh": peer(r)}, device_id_type=MESH)


    piece = 2 * tokens // PARTS

    def main_copy(t, part):
        span = pl.ds(part * piece, piece)
        return pltpu.make_async_remote_copy(
            src_ref=kv.at[2 * t, span], dst_ref=kv.at[2 * t + 2, span],
            send_sem=main_send.at[t, part], recv_sem=main_recv.at[t, part],
            device_id={"seq": seq_at(2)}, device_id_type=MESH)

    def aux_copy(u, src, step):
        return pltpu.make_async_remote_copy(
            src_ref=kv.at[src], dst_ref=kv.at[2 * u + 1],
            send_sem=aux_send.at[u], recv_sem=aux_recv.at[u],
            device_id={"seq": seq_at(step)}, device_id_type=MESH)

    def far_copy(part):
        span = pl.ds(part * piece, piece)
        m = RUN - chip
        return pltpu.make_async_remote_copy(
            src_ref=kv.at[0, span], dst_ref=kv.at[2 * m, span],
            send_sem=far_send.at[0, part], recv_sem=main_recv.at[m - 1, part],
            device_id={"seq": seq_at(2 * m)}, device_id_type=MESH)

    def far_odd_copy():
        return pltpu.make_async_remote_copy(
            src_ref=kv.at[0], dst_ref=kv.at[2 * last + 1],
            send_sem=far_send.at[1, 0], recv_sem=aux_recv.at[last],
            device_id={"seq": seq_at(2 * last + 1)}, device_id_type=MESH)

    hold = jnp.where((my_hi == 0) & (chip < last), half, 0)

    def chunk(i):
        return jnp.where(i < hold, half + i, jnp.where(i < hold + half, i - hold, i))

    first_r = chunk(0)
    lead_row = pl.multiple_of(peer(first_r) * rows, rows)
    group = heads // PARTS

    def seen(b):
        return b * tokens <= base - first

    def lead(blocks, part):
        fresh = blocks[0] == 0
        where = pl.ds(part * group * rows, group * rows)
        q = jnp.concatenate(
            [qv[pl.ds(lead_row, rows), h * HEAD:(h + 1) * HEAD]
             for h in range(part * group, (part + 1) * group)], axis=0)
        scores = []
        for b in blocks:
            s = lax.dot_general(q, kv[b, :tokens], (((1,), (1,)), ((), ())),
                                preferred_element_type=jnp.float32)
            if b == 0:
                token = lead_row + lax.rem(lax.broadcasted_iota(jnp.int32, s.shape, 0), rows)
                s = jnp.where(lax.broadcasted_iota(jnp.int32, s.shape, 1) <= token, s, LOW)
            scores.append(s)
        old = jnp.full((group * rows, HEAD), LOW, jnp.float32) if fresh else peak_scr[where, :]
        best = old[:, :1]
        for b, s in zip(blocks, scores):
            top = jnp.max(s, axis=1, keepdims=True)
            best = jnp.maximum(best, top if b == 0 else jnp.where(seen(b), top, LOW))
        total = jnp.zeros((group * rows, HEAD), jnp.float32)
        acc = jnp.zeros((group * rows, HEAD), jnp.float32)
        for b, s in zip(blocks, scores):
            shift = best if b == 0 else jnp.where(seen(b), best, -LOW)
            p = jnp.exp2((s - shift) * EXP2_SCALE)
            for j in range(tokens // HEAD):
                total = total + p[:, j * HEAD:(j + 1) * HEAD]
            acc = acc + jnp.dot(p.astype(jnp.bfloat16), kv[b, tokens:], preferred_element_type=jnp.float32)
        if not fresh:
            shrink = jnp.exp2((old - best) * EXP2_SCALE)
            total = total + total_scr[where, :] * shrink
            acc = acc + acc_scr[where, :] * shrink
        peak_scr[where, :] = jnp.broadcast_to(best, (group * rows, HEAD))
        total_scr[where, :] = total
        acc_scr[where, :] = acc

    def aux_wait(u):
        aux_copy(u, 0, 1).wait_recv()

    for t in range(last + 1):
        for part in range(PARTS):
            if t > 0:
                main_copy(t - 1, part).wait_recv()
            if t == 0:
                main_copy(t, part).start()
            elif t < last:
                @pl.when(chip < RUN - 1)
                def _():
                    main_copy(t, part).start()
            for m in range(2, last + 1):
                if t == FAR_STEP[m - 2]:
                    @pl.when(chip == RUN - m)
                    def _():
                        far_copy(part).start()
            if part == PARTS - 1:
                if t == 0:
                    @pl.when(core == 0)
                    def _():
                        aux_copy(0, 0, 1).start()
                else:
                    aux_copy(t - core, 2 * t, 1 - 2 * core).start()
                if t == last:
                    @pl.when(tail)
                    def _():
                        aux_copy(last, 2 * last, 1).start()
                if t == FAR_STEP[-1]:
                    @pl.when(far_odd)
                    def _():
                        far_odd_copy().start()
            if t > 0:
                if t > 1 and part == 0:
                    aux_wait(t - 2)
                lead((0,) if t == 1 else (2 * t - 2, 2 * t - 3), part)
        if t == 0:
            local[2].wait()
            local[3].wait()
            base = me * tokens
            first = jnp.int32(0)
            start = jnp.int32(0)
            for a in range(lens.shape[0]):
                first = jnp.where(start <= base, start, first)
                start = start + lens[a]

    for blocks in ((SPAN - 2, SPAN - 3), (SPAN - 1,)):
        aux_wait((blocks[-1] - 1) // 2)
        for part in range(PARTS):
            lead(blocks, part)

    def attend(row0):
        q = jnp.concatenate(
            [qv[pl.ds(row0, rows), h * HEAD:(h + 1) * HEAD] for h in range(heads)], axis=0)
        peak = jnp.full((heads * rows, HEAD), LOW, jnp.float32)
        for b in range(SPAN):
            s = lax.dot_general(q, kv[b, :tokens], (((1,), (1,)), ((), ())),
                                preferred_element_type=jnp.float32)
            if b == 0:
                token = row0 + lax.rem(lax.broadcasted_iota(jnp.int32, s.shape, 0), rows)
                s = jnp.where(lax.broadcasted_iota(jnp.int32, s.shape, 1) <= token, s, LOW)
            s_scr[:, b * tokens:(b + 1) * tokens] = s
            best = s[:, :HEAD]
            for j in range(1, tokens // HEAD):
                best = jnp.maximum(best, s[:, j * HEAD:(j + 1) * HEAD])
            if b > 0:
                best = jnp.where(seen(b), best, LOW)
            peak = jnp.maximum(peak, best)
        peak = jnp.max(peak, axis=1, keepdims=True)
        total = jnp.zeros((heads * rows, HEAD), jnp.float32)
        acc = jnp.zeros((heads * rows, HEAD), jnp.float32)
        for b in range(SPAN):
            shift = peak if b == 0 else jnp.where(seen(b), peak, -LOW)
            p = jnp.exp2((s_scr[:, b * tokens:(b + 1) * tokens] - shift) * EXP2_SCALE)
            for j in range(tokens // HEAD):
                total = total + p[:, j * HEAD:(j + 1) * HEAD]
            acc = acc + jnp.dot(p.astype(jnp.bfloat16), kv[b, tokens:], preferred_element_type=jnp.float32)
        return (acc / jnp.sum(total, axis=1, keepdims=True)).astype(jnp.bfloat16)

    columns = pl.ds(pl.multiple_of(mine * width, width), width)

    def out_copy(r):
        return pltpu.make_async_remote_copy(
            src_ref=stage.at[r], dst_ref=out_hbm.at[:, columns],
            send_sem=out_send.at[r], recv_sem=out_recv.at[r],
            device_id={"kvh": peer(r)}, device_id_type=MESH)

    def finish(r, done):
        for h in range(heads):
            stage[r, :, h * HEAD:(h + 1) * HEAD] = done[h * rows:(h + 1) * rows, :]

        @pl.when(r < n_kvh - 1)
        def _():
            out_copy(r).start()

    @pl.when(my_hi == 0)
    def _():
        pl.semaphore_wait(ready, half)

    finish(first_r, (acc_scr[...] / jnp.sum(total_scr[...], axis=1, keepdims=True)).astype(jnp.bfloat16))

    def one_chunk(i, carry):
        r = chunk(i)
        target = jnp.where(r == n_kvh - 1, mine, peer(r))
        finish(r, attend(pl.multiple_of(target * rows, rows)))
        return carry

    lax.fori_loop(1, n_kvh, one_chunk, 0)
    self_copy = pltpu.make_async_copy(stage.at[n_kvh - 1], out_hbm.at[:, columns], local_sem.at[0])
    self_copy.start()
    self_copy.wait()
    for r in range(n_kvh - 1):
        out_copy(r).wait()
    for part in range(PARTS):
        main_copy(0, part).wait_send()

        @pl.when(chip < RUN - 1)
        def _():
            for t in range(1, last):
                main_copy(t, part).wait_send()

        @pl.when(far_even)
        def _():
            far_copy(part).wait_send()

    for u in range(last):
        aux_copy(u, 0, 1).wait_send()

    @pl.when((core == 0) | tail)
    def _():
        aux_copy(last, 0, 1).wait_send()

    @pl.when(far_odd)
    def _():
        far_odd_copy().wait_send()


def shards(queries, keys, values, answer_lengths):
    tokens, width = queries.shape
    n_seq, n_kvh = lax.axis_size("seq"), lax.axis_size("kvh")
    rows = tokens // n_kvh
    heads = width // HEAD
    dma = pltpu.SemaphoreType.DMA
    hbm_spec = pl.BlockSpec(memory_space=pltpu.HBM)
    return pl.pallas_call(
        functools.partial(kernel, n_seq, n_kvh),
        out_shape=jax.ShapeDtypeStruct((rows, n_kvh * width), jnp.bfloat16),
        in_specs=[hbm_spec] * 4,
        out_specs=pl.BlockSpec(memory_space=pl.ANY),
        scratch_shapes=[
            pltpu.SMEM(answer_lengths.shape, jnp.int32),
            pltpu.VMEM((tokens, width), jnp.bfloat16),
            pltpu.VMEM((SPAN, 2 * tokens, HEAD), jnp.bfloat16),
            pltpu.VMEM((heads * rows, SPAN * tokens), jnp.float32),
            pltpu.VMEM((n_kvh, rows, width), jnp.bfloat16),
            pltpu.VMEM((heads * rows, HEAD), jnp.float32),
            pltpu.VMEM((heads * rows, HEAD), jnp.float32),
            pltpu.VMEM((heads * rows, HEAD), jnp.float32),
            dma((4,)),
            dma((SPAN // 2, PARTS)),
            dma((SPAN // 2, PARTS)),
            dma((SPAN // 2,)),
            dma((SPAN // 2,)),
            dma((2, PARTS)),
            dma((n_kvh,)),
            dma((n_kvh,)),
            pltpu.SemaphoreType.REGULAR,
        ],
        compiler_params=pltpu.CompilerParams(
            collective_id=0, has_side_effects=True, vmem_limit_bytes=63 * 1024 * 1024),
        cost_estimate=pl.CostEstimate(
            flops=4 * tokens * width * SPAN * tokens,
            bytes_accessed=4 * tokens * width,
            transcendentals=tokens * heads * SPAN * tokens),
    )(answer_lengths, queries, keys, values)


def solution(mesh):
    in_specs = (P("seq", "kvh"), P("seq", "kvh"), P("seq", "kvh"), P())
    out_specs = P(("seq", "kvh"), None)
    return jax.shard_map(shards, mesh=mesh, in_specs=in_specs, out_specs=out_specs, check_vma=False)
```

```python
import functools
import math

import jax
import jax.numpy as jnp
from jax import lax
from jax.experimental import pallas as pl
from jax.experimental.pallas import tpu as pltpu
from jax.sharding import PartitionSpec as P

HEAD = 128
SPAN = 12
PARTS = 4
RUN = 8
FAR_STEP = (0, 0, 0, 0, 0)
MESH = pl.DeviceIdType.MESH
LOW = -1e30
EXP2_SCALE = math.log2(math.e) / math.sqrt(HEAD)


def kernel(n_seq, n_kvh, len_hbm, q_hbm, k_hbm, v_hbm, out_hbm, lens, qv, kv, s_scr, stage, peak_scr, total_scr, acc_scr,
           local_sem, main_send, main_recv, aux_send, aux_recv, far_send, out_send, out_recv, ready):
    tokens, width = qv.shape
    heads = width // HEAD
    rows = tokens // n_kvh
    half = n_kvh // 2
    me = lax.axis_index("seq")
    mine = lax.axis_index("kvh")
    core = lax.rem(me, 2)
    chip = lax.rem(me // 2, RUN)
    last = SPAN // 2 - 1
    my_hi = mine // half
    my_lo = lax.rem(mine, half)

    def seq_at(step):
        return lax.rem(me + (step + n_seq), n_seq)

    def peer(r):
        cross = r < half
        hi = jnp.where(cross, 1 - my_hi, my_hi)
        lo = lax.rem(my_lo + jnp.where(cross, r, r - half + 1), half)
        return hi * half + lo

    local = [
        pltpu.make_async_copy(k_hbm, kv.at[0, :tokens], local_sem.at[0]),
        pltpu.make_async_copy(v_hbm, kv.at[0, tokens:], local_sem.at[1]),
        pltpu.make_async_copy(q_hbm, qv, local_sem.at[2]),
        pltpu.make_async_copy(len_hbm, lens, local_sem.at[3]),
    ]
    for copy in local:
        copy.start()

    barrier = pltpu.get_barrier_semaphore()
    greets = [(-2, core >= 0), (1 - 2 * core, core >= 0), (-1, (core == 0) & (chip > 0))]
    greets += [(-2 * m, chip == 0) for m in range(2, last + 1)]
    greets += [(-2 * last - 1, (core == 0) & (chip == 0))]
    for step, known in greets:
        @pl.when(known)
        def _():
            pl.semaphore_signal(barrier, inc=1, device_id={"seq": seq_at(step)}, device_id_type=MESH)
    tail = (core == 1) & (chip < RUN - 1)
    far_even = (chip >= RUN - last) & (chip < RUN - 1)
    far_odd = (core == 1) & (chip == RUN - last - 1)
    greeted = half - 1 + my_hi * half + 2
    for known in (tail, far_even, far_odd):
        greeted = greeted + known.astype(jnp.int32)

    for r in range(half, n_kvh - 1):
        pl.semaphore_signal(barrier, inc=1, device_id={"kvh": peer(r)}, device_id_type=MESH)

    @pl.when(my_hi == 0)
    def _():
        for r in range(half):
            pl.semaphore_signal(barrier, inc=1, device_id={"kvh": peer(r)}, device_id_type=MESH)

    local[0].wait()
    local[1].wait()
    pl.semaphore_wait(barrier, greeted)

    @pl.when(my_hi == 1)
    def _():
        for r in range(half):
            pl.semaphore_signal(ready, inc=1, device_id={"kvh": peer(r)}, device_id_type=MESH)


    piece = 2 * tokens // PARTS

    def main_copy(t, part):
        span = pl.ds(part * piece, piece)
        return pltpu.make_async_remote_copy(
            src_ref=kv.at[2 * t, span], dst_ref=kv.at[2 * t + 2, span],
            send_sem=main_send.at[t, part], recv_sem=main_recv.at[t, part],
            device_id={"seq": seq_at(2)}, device_id_type=MESH)

    def aux_copy(u, src, step):
        return pltpu.make_async_remote_copy(
            src_ref=kv.at[src], dst_ref=kv.at[2 * u + 1],
            send_sem=aux_send.at[u], recv_sem=aux_recv.at[u],
            device_id={"seq": seq_at(step)}, device_id_type=MESH)

    def far_copy(part):
        span = pl.ds(part * piece, piece)
        m = RUN - chip
        return pltpu.make_async_remote_copy(
            src_ref=kv.at[0, span], dst_ref=kv.at[2 * m, span],
            send_sem=far_send.at[0, part], recv_sem=main_recv.at[m - 1, part],
            device_id={"seq": seq_at(2 * m)}, device_id_type=MESH)

    def far_odd_copy():
        return pltpu.make_async_remote_copy(
            src_ref=kv.at[0], dst_ref=kv.at[2 * last + 1],
            send_sem=far_send.at[1, 0], recv_sem=aux_recv.at[last],
            device_id={"seq": seq_at(2 * last + 1)}, device_id_type=MESH)

    hold = jnp.where(my_hi == 0, half, 0)

    def chunk(i):
        return jnp.where(i < hold, half + i, jnp.where(i < hold + half, i - hold, i))

    first_r = chunk(0)
    lead_row = pl.multiple_of(peer(first_r) * rows, rows)
    group = heads // PARTS

    def seen(b):
        return b * tokens <= base - first

    def lead(blocks, part):
        fresh = blocks[0] == 0
        where = pl.ds(part * group * rows, group * rows)
        q = jnp.concatenate(
            [qv[pl.ds(lead_row, rows), h * HEAD:(h + 1) * HEAD]
             for h in range(part * group, (part + 1) * group)], axis=0)
        scores = []
        for b in blocks:
            s = lax.dot_general(q, kv[b, :tokens], (((1,), (1,)), ((), ())),
                                preferred_element_type=jnp.float32)
            if b == 0:
                token = lead_row + lax.rem(lax.broadcasted_iota(jnp.int32, s.shape, 0), rows)
                s = jnp.where(lax.broadcasted_iota(jnp.int32, s.shape, 1) <= token, s, LOW)
            scores.append(s)
        old = jnp.full((group * rows, HEAD), LOW, jnp.float32) if fresh else peak_scr[where, :]
        best = old[:, :1]
        for b, s in zip(blocks, scores):
            top = jnp.max(s, axis=1, keepdims=True)
            best = jnp.maximum(best, top if b == 0 else jnp.where(seen(b), top, LOW))
        total = jnp.zeros((group * rows, HEAD), jnp.float32)
        acc = jnp.zeros((group * rows, HEAD), jnp.float32)
        for b, s in zip(blocks, scores):
            shift = best if b == 0 else jnp.where(seen(b), best, -LOW)
            p = jnp.exp2((s - shift) * EXP2_SCALE)
            for j in range(tokens // HEAD):
                total = total + p[:, j * HEAD:(j + 1) * HEAD]
            acc = acc + jnp.dot(p.astype(jnp.bfloat16), kv[b, tokens:], preferred_element_type=jnp.float32)
        if not fresh:
            shrink = jnp.exp2((old - best) * EXP2_SCALE)
            total = total + total_scr[where, :] * shrink
            acc = acc + acc_scr[where, :] * shrink
        peak_scr[where, :] = jnp.broadcast_to(best, (group * rows, HEAD))
        total_scr[where, :] = total
        acc_scr[where, :] = acc

    def aux_wait(u):
        aux_copy(u, 0, 1).wait_recv()

    for t in range(last + 1):
        for part in range(PARTS):
            if t > 0:
                main_copy(t - 1, part).wait_recv()
            if t == 0:
                main_copy(t, part).start()
            elif t < last:
                @pl.when(chip < RUN - 1)
                def _():
                    main_copy(t, part).start()
            for m in range(2, last + 1):
                if t == FAR_STEP[m - 2]:
                    @pl.when(chip == RUN - m)
                    def _():
                        far_copy(part).start()
            if part == PARTS - 1:
                if t == 0:
                    @pl.when(core == 0)
                    def _():
                        aux_copy(0, 0, 1).start()
                else:
                    aux_copy(t - core, 2 * t, 1 - 2 * core).start()
                if t == last:
                    @pl.when(tail)
                    def _():
                        aux_copy(last, 2 * last, 1).start()
                if t == FAR_STEP[-1]:
                    @pl.when(far_odd)
                    def _():
                        far_odd_copy().start()
            if t > 0:
                if t > 1 and part == 0:
                    aux_wait(t - 2)
                lead((0,) if t == 1 else (2 * t - 2, 2 * t - 3), part)
        if t == 0:
            local[2].wait()
            local[3].wait()
            base = me * tokens
            first = jnp.int32(0)
            start = jnp.int32(0)
            for a in range(lens.shape[0]):
                first = jnp.where(start <= base, start, first)
                start = start + lens[a]

    for blocks in ((SPAN - 2, SPAN - 3), (SPAN - 1,)):
        aux_wait((blocks[-1] - 1) // 2)
        for part in range(PARTS):
            lead(blocks, part)

    def attend_heads(row0, part):
        where = pl.ds(part * group * rows, group * rows)
        q = jnp.concatenate(
            [qv[pl.ds(row0, rows), h * HEAD:(h + 1) * HEAD] for h in range(part * group, (part + 1) * group)], axis=0)
        peak = jnp.full((group * rows, HEAD), LOW, jnp.float32)
        for b in range(SPAN):
            s = lax.dot_general(q, kv[b, :tokens], (((1,), (1,)), ((), ())),
                                preferred_element_type=jnp.float32)
            if b == 0:
                token = row0 + lax.rem(lax.broadcasted_iota(jnp.int32, s.shape, 0), rows)
                s = jnp.where(lax.broadcasted_iota(jnp.int32, s.shape, 1) <= token, s, LOW)
            s_scr[where, b * tokens:(b + 1) * tokens] = s
            best = s[:, :HEAD]
            for j in range(1, tokens // HEAD):
                best = jnp.maximum(best, s[:, j * HEAD:(j + 1) * HEAD])
            if b > 0:
                best = jnp.where(seen(b), best, LOW)
            peak = jnp.maximum(peak, best)
        peak = jnp.max(peak, axis=1, keepdims=True)
        total = jnp.zeros((group * rows, HEAD), jnp.float32)
        acc = jnp.zeros((group * rows, HEAD), jnp.float32)
        for b in range(SPAN):
            shift = peak if b == 0 else jnp.where(seen(b), peak, -LOW)
            p = jnp.exp2((s_scr[where, b * tokens:(b + 1) * tokens] - shift) * EXP2_SCALE)
            for j in range(tokens // HEAD):
                total = total + p[:, j * HEAD:(j + 1) * HEAD]
            acc = acc + jnp.dot(p.astype(jnp.bfloat16), kv[b, tokens:], preferred_element_type=jnp.float32)
        return (acc / jnp.sum(total, axis=1, keepdims=True)).astype(jnp.bfloat16)

    def attend(row0):
        return jnp.concatenate([attend_heads(row0, part) for part in range(PARTS)], axis=0)

    columns = pl.ds(pl.multiple_of(mine * width, width), width)

    def out_copy(r):
        return pltpu.make_async_remote_copy(
            src_ref=stage.at[r], dst_ref=out_hbm.at[:, columns],
            send_sem=out_send.at[r], recv_sem=out_recv.at[r],
            device_id={"kvh": peer(r)}, device_id_type=MESH)

    def finish(r, done):
        for h in range(heads):
            stage[r, :, h * HEAD:(h + 1) * HEAD] = done[h * rows:(h + 1) * rows, :]

        @pl.when(r < n_kvh - 1)
        def _():
            out_copy(r).start()

    @pl.when(my_hi == 0)
    def _():
        pl.semaphore_wait(ready, half)

    finish(first_r, (acc_scr[...] / jnp.sum(total_scr[...], axis=1, keepdims=True)).astype(jnp.bfloat16))

    def one_chunk(i, carry):
        r = chunk(i)
        target = jnp.where(r == n_kvh - 1, mine, peer(r))
        finish(r, attend(pl.multiple_of(target * rows, rows)))
        return carry

    lax.fori_loop(1, n_kvh, one_chunk, 0)
    self_copy = pltpu.make_async_copy(stage.at[n_kvh - 1], out_hbm.at[:, columns], local_sem.at[0])
    self_copy.start()
    self_copy.wait()
    for r in range(n_kvh - 1):
        out_copy(r).wait()
    for part in range(PARTS):
        main_copy(0, part).wait_send()

        @pl.when(chip < RUN - 1)
        def _():
            for t in range(1, last):
                main_copy(t, part).wait_send()

        @pl.when(far_even)
        def _():
            far_copy(part).wait_send()

    for u in range(last):
        aux_copy(u, 0, 1).wait_send()

    @pl.when((core == 0) | tail)
    def _():
        aux_copy(last, 0, 1).wait_send()

    @pl.when(far_odd)
    def _():
        far_odd_copy().wait_send()


def shards(queries, keys, values, answer_lengths):
    tokens, width = queries.shape
    n_seq, n_kvh = lax.axis_size("seq"), lax.axis_size("kvh")
    rows = tokens // n_kvh
    heads = width // HEAD
    dma = pltpu.SemaphoreType.DMA
    hbm_spec = pl.BlockSpec(memory_space=pltpu.HBM)
    return pl.pallas_call(
        functools.partial(kernel, n_seq, n_kvh),
        out_shape=jax.ShapeDtypeStruct((rows, n_kvh * width), jnp.bfloat16),
        in_specs=[hbm_spec] * 4,
        out_specs=pl.BlockSpec(memory_space=pl.ANY),
        scratch_shapes=[
            pltpu.SMEM(answer_lengths.shape, jnp.int32),
            pltpu.VMEM((tokens, width), jnp.bfloat16),
            pltpu.VMEM((SPAN, 2 * tokens, HEAD), jnp.bfloat16),
            pltpu.VMEM((heads * rows, SPAN * tokens), jnp.float32),
            pltpu.VMEM((n_kvh, rows, width), jnp.bfloat16),
            pltpu.VMEM((heads * rows, HEAD), jnp.float32),
            pltpu.VMEM((heads * rows, HEAD), jnp.float32),
            pltpu.VMEM((heads * rows, HEAD), jnp.float32),
            dma((4,)),
            dma((SPAN // 2, PARTS)),
            dma((SPAN // 2, PARTS)),
            dma((SPAN // 2,)),
            dma((SPAN // 2,)),
            dma((2, PARTS)),
            dma((n_kvh,)),
            dma((n_kvh,)),
            pltpu.SemaphoreType.REGULAR,
        ],
        compiler_params=pltpu.CompilerParams(
            collective_id=0, has_side_effects=True, vmem_limit_bytes=63 * 1024 * 1024),
        cost_estimate=pl.CostEstimate(
            flops=4 * tokens * width * SPAN * tokens,
            bytes_accessed=4 * tokens * width,
            transcendentals=tokens * heads * SPAN * tokens),
    )(answer_lengths, queries, keys, values)


def solution(mesh):
    in_specs = (P("seq", "kvh"), P("seq", "kvh"), P("seq", "kvh"), P())
    out_specs = P(("seq", "kvh"), None)
    return jax.shard_map(shards, mesh=mesh, in_specs=in_specs, out_specs=out_specs, check_vma=False)
```
